256 devices in a mesh: ctx: 32 (over y, x, core), head: 8 (over z).
Axes of the slice: x: 4, y: 4, z: 8, core: 2. Of those that a mesh axis runs over, the one named last changes fastest.
Arguments:
- queries: bfloat16 [4096, 24576], P('ctx', 'head'), may hold values from -120 to 120
- latents: bfloat16 [4096, 576], P('ctx'), may hold values from -6 to 6
- w_uk: bfloat16 [512, 16384], P(None, 'head'), may hold values from -0.5 to 0.5
- w_uv: bfloat16 [512, 16384], P(None, 'head'), may hold values from -0.25 to 0.25
- out_grad: bfloat16 [4096, 16384], P('ctx', 'head'), may hold values from -6 to 6
- doc_ids: int32 [4096], P('ctx'), may hold values from 0 to 8192, as said below
Outputs:
- attn_output: bfloat16 [4096, 16384], P('ctx', 'head')
- query_grad: float32 [4096, 24576], P('ctx', 'head')
- latent_grad: float32 [4096, 576], P('ctx')
- w_uk_grad: float32 [512, 16384], P('ctx', 'head')
- w_uv_grad: float32 [512, 16384], P('ctx', 'head')
The draws below stay inside these ranges and needn't reach their ends.
Inputs may be any that keep to these rules, and one draw needn't show every extreme that they name: `doc_ids`: document numbers never fall along the window; every document is a run of 1 to 448 tokens, and one holds exactly 448.
All inputs are finite; a program needn't handle non-finite values.
Results may differ from the reference program's by a relative error of at most 0.012.
Values may be sent and summed in bfloat16 or wider, within the bound.
No kernel may reach another device: no remote copies, remote signals or barrier semaphores. Data moves between devices by JAX's collectives and lax.ppermute only.
A program may use at most 128 MiB of HBM per device.

```python
import jax
import jax.numpy as jnp
from jax import lax

HEADS = 128
LATENT = 512
ROPE = 64
NOPE = 128
TOK_DEV = 128
SPAN = 4
TOKENS = 4096
MOST_DOC = 448
MIN_DOC = 32
N_CTX = 32


def rope_keys(key):
    return jax.random.normal(jax.random.fold_in(key, 11), (TOKENS, ROPE), jnp.float32)


def draw_latents(key, part):
    shared = rope_keys(key)
    key = jax.random.fold_in(key, 3)
    latent_part = jax.random.normal(key, (TOKENS, LATENT), jnp.float32)
    joined = jnp.concatenate([latent_part, shared], axis=1)
    return jnp.clip(joined, -6.0, 6.0).astype(jnp.bfloat16)


def draw_queries(key, part):
    key = jax.random.fold_in(key, 4)
    values = jax.random.normal(key, (TOKENS, HEADS, NOPE + ROPE), jnp.float32)
    values = jnp.clip(values, -120.0, 120.0)
    return values.reshape(TOKENS, HEADS * (NOPE + ROPE)).astype(jnp.bfloat16)


def draw_doc_ids(key, part):
    key = jax.random.fold_in(key, 7)
    half_rows = TOK_DEV // 2
    block_at = jax.random.randint(jax.random.fold_in(key, 1), (), 0, N_CTX - SPAN)
    offset = jax.random.randint(jax.random.fold_in(key, 2), (), 1, half_rows)
    start_long = block_at * TOK_DEV + half_rows + offset
    first_len = jax.random.randint(jax.random.fold_in(key, 3), (TOKENS,), MIN_DOC, MOST_DOC + 1)
    second_len = jax.random.randint(jax.random.fold_in(key, 4), (TOKENS,), MIN_DOC, MOST_DOC + 1)
    first_end = jnp.cumsum(first_len)
    second_end = jnp.cumsum(second_len)
    position = jnp.arange(TOKENS, dtype=jnp.int32)
    tail_len = TOKENS - start_long - MOST_DOC
    before = jnp.searchsorted(first_end, position, side='right').astype(jnp.int32)
    ends_inside = jnp.searchsorted(second_end, tail_len, side='left').astype(jnp.int32)
    after_ids = jnp.searchsorted(second_end, position - start_long - MOST_DOC, side='right').astype(jnp.int32)
    tail_numbers = 2 * TOKENS - (ends_inside - after_ids)
    doc_numbers = jnp.where(position < start_long, before, jnp.where(position < start_long + MOST_DOC, TOKENS, tail_numbers))
    return doc_numbers.astype(jnp.int32)


def block_levels(rng, shape, cuts, least, top_value):
    loudness = 1.0
    for dim, blocks in cuts:
        steps = jax.random.uniform(jax.random.fold_in(jax.random.fold_in(rng, 6), dim), (blocks,), jnp.float32, least / len(cuts), top_value / len(cuts))
        loudness = loudness * jnp.repeat(jnp.exp(steps), shape[dim] // blocks).reshape((-1,) + (1,) * (len(shape) - 1 - dim))
    return loudness


def normal_values(key, extent, scale, most, split=(), kind=jnp.bfloat16):
    gain = block_levels(key, extent, split, -0.22, 0.18) if split else 1.0
    result = jax.random.normal(key, extent, jnp.float32) * scale * gain
    return jnp.minimum(jnp.maximum(result, -most), most).astype(kind)


def setup_inputs(seed: int = 0) -> dict:
    key_of = jax.random.split(jax.random.key(seed), 7)
    return {
        "queries": draw_queries(jax.random.fold_in(key_of[6], 71), 0),
        "latents": draw_latents(jax.random.fold_in(key_of[6], 71), 0),
        "w_uk": normal_values(key_of[2], (LATENT, HEADS * NOPE), NOPE ** -0.5, 0.5, ((1, 8),)),
        "w_uv": normal_values(key_of[3], (LATENT, HEADS * NOPE), LATENT ** -0.5, 0.25, ((1, 8),)),
        "out_grad": normal_values(key_of[4], (TOKENS, HEADS * NOPE), 1.0, 6.0, ((0, 32), (1, 8))),
        "doc_ids": draw_doc_ids(jax.random.fold_in(key_of[6], 71), 0),
    }


masked_value = -1e30


def to_float(array):
    return array.astype(jnp.float32)


def attend(query_blk, grad_blk, key_rows, visible, w_uk, w_uv):
    head_count = query_blk.shape[1]
    q_nope = query_blk[:, :, :NOPE]
    q_rope = query_blk[:, :, NOPE:]
    c_nope = key_rows[:, :LATENT]
    k_rope = key_rows[:, LATENT:]
    up_key = w_uk.reshape(LATENT, head_count, NOPE)
    up_value = w_uv.reshape(LATENT, head_count, NOPE)
    softmax_scale = (NOPE + ROPE) ** -0.5
    absorbed = jnp.einsum('thd,lhd->thl', to_float(q_nope), to_float(up_key)).astype(jnp.bfloat16)
    scores = (jnp.einsum('thl,ul->thu', to_float(absorbed), to_float(c_nope))
              + jnp.einsum('thr,ur->thu', to_float(q_rope), to_float(k_rope))) * softmax_scale
    allowed = visible[:, None, :]
    scores = jnp.where(allowed, scores, masked_value)
    top_score = jnp.max(scores, axis=-1, keepdims=True)
    exp_terms = jnp.where(allowed, jnp.exp(scores - top_score), 0.0)
    attn_probs = exp_terms / jnp.sum(exp_terms, axis=-1, keepdims=True)
    probs_bf = attn_probs.astype(jnp.bfloat16)
    attended = jnp.einsum('thu,ul->thl', to_float(probs_bf), to_float(c_nope)).astype(jnp.bfloat16)
    attn_out = jnp.einsum('thl,lhd->thd', to_float(attended), to_float(up_value)).astype(jnp.bfloat16)
    grad_latent = jnp.einsum('thd,lhd->thl', to_float(grad_blk), to_float(up_value)).astype(jnp.bfloat16)
    grad_probs = jnp.einsum('thl,ul->thu', to_float(grad_latent), to_float(c_nope))
    row_delta = jnp.sum(attn_probs * grad_probs, axis=-1, keepdims=True)
    grad_scores = (attn_probs * (grad_probs - row_delta) * softmax_scale).astype(jnp.bfloat16)
    grad_absorbed = jnp.einsum('thu,ul->thl', to_float(grad_scores), to_float(c_nope)).astype(jnp.bfloat16)
    grad_qrope = jnp.einsum('thu,ur->thr', to_float(grad_scores), to_float(k_rope))
    grad_qnope = jnp.einsum('thl,lhd->thd', to_float(grad_absorbed), to_float(up_key))
    grad_query = jnp.concatenate([grad_qnope, grad_qrope], axis=-1)
    grad_cnope = (jnp.einsum('thu,thl->ul', to_float(probs_bf), to_float(grad_latent))
                  + jnp.einsum('thu,thl->ul', to_float(grad_scores), to_float(absorbed)))
    grad_krope = jnp.einsum('thu,thr->ur', to_float(grad_scores), to_float(q_rope))
    grad_keys = jnp.concatenate([grad_cnope, grad_krope], axis=-1)
    return attn_out, grad_query, grad_keys, grad_absorbed, attended, q_nope


def reference(queries, latents, w_uk, w_uv, out_grad, doc_ids):
    head_count = w_uk.shape[1] // NOPE
    margin = SPAN * TOK_DEV
    key_width = LATENT + ROPE
    padded_lat = jnp.concatenate([jnp.zeros((margin, key_width), jnp.bfloat16), latents], axis=0)
    padded_ids = jnp.concatenate([jnp.full((margin,), -1, jnp.int32), doc_ids.astype(jnp.int32)], axis=0)
    query_blocks = queries.reshape(N_CTX, TOK_DEV, head_count, NOPE + ROPE)
    grad_blocks = out_grad.reshape(N_CTX, TOK_DEV, head_count, NOPE)
    id_blocks = doc_ids.astype(jnp.int32).reshape(N_CTX, TOK_DEV)

    def one_block(state_now, inputs):
        grad_pad, grad_wk, grad_wv = state_now
        query_blk, grad_blk, query_ids, block_no = inputs
        first_row = (block_no * TOK_DEV).astype(jnp.int32)
        key_rows = lax.dynamic_slice_in_dim(padded_lat, first_row, margin + TOK_DEV, 0)
        key_ids = lax.dynamic_slice_in_dim(padded_ids, first_row, margin + TOK_DEV, 0)
        query_pos = first_row + jnp.arange(TOK_DEV, dtype=jnp.int32)
        key_pos = first_row - margin + jnp.arange(margin + TOK_DEV, dtype=jnp.int32)
        visible = (key_ids[None, :] == query_ids[:, None]) & (key_pos[None, :] <= query_pos[:, None])
        attn_out, grad_query, grad_keys, grad_absorbed, attended, q_nope = attend(
            query_blk, grad_blk, key_rows, visible, w_uk, w_uv)
        current = lax.dynamic_slice_in_dim(grad_pad, first_row, margin + TOK_DEV, 0)
        grad_pad = lax.dynamic_update_slice_in_dim(grad_pad, current + grad_keys, first_row, 0)
        grad_wk = grad_wk + jnp.einsum('thl,thd->lhd', to_float(grad_absorbed), to_float(q_nope)).reshape(LATENT, head_count * NOPE)
        grad_wv = grad_wv + jnp.einsum('thl,thd->lhd', to_float(attended), to_float(grad_blk)).reshape(LATENT, head_count * NOPE)
        return (grad_pad, grad_wk, grad_wv), (attn_out, grad_query)

    initial = (jnp.zeros((margin + TOKENS, key_width), jnp.float32),
               jnp.zeros((LATENT, head_count * NOPE), jnp.float32),
               jnp.zeros((LATENT, head_count * NOPE), jnp.float32))
    final_state, stacked = lax.scan(one_block, initial,
                                    (query_blocks, grad_blocks, id_blocks, jnp.arange(N_CTX, dtype=jnp.int32)))
    grad_pad, grad_wk, grad_wv = final_state
    attn_outs, query_grads = stacked
    return (attn_outs.reshape(TOKENS, head_count * NOPE),
            query_grads.reshape(TOKENS, head_count * (NOPE + ROPE)),
            grad_pad[margin:],
            grad_wk,
            grad_wv)
```

```python
import functools

import jax
import jax.numpy as jnp
from jax import lax
from jax.experimental import pallas as pl
from jax.experimental.pallas import tpu as pltpu
from jax.sharding import PartitionSpec as P

LATENT = 512
ROPE = 64
NOPE = 128
WIDE = LATENT + ROPE
QDIM = NOPE + ROPE
SPAN = 4
TOK = 128
HALF = 64
BACK = 448
WINDOW = BACK + TOK
SEEN = BACK + HALF
PACKED = 640
N_CTX = 32
CHUNK = LATENT // N_CTX
HIDDEN = -1e30

bf16 = jnp.bfloat16
f32 = jnp.float32


def dot(a, b, ca=1, cb=0):
    return lax.dot_general(a, b, (((ca,), (cb,)), ((), ())), preferred_element_type=f32)


def place(i):
    return i // 8, (i // 2) % 4, i % 2


def index_of(y, x, c):
    return (y * 4 + x) * 2 + c


NEAR = {0: 1, 1: 0, 2: 3, 3: 2}
FAR = {0: 3, 3: 0, 1: 2, 2: 1}


def halving_pairs(stream):
    order = (NEAR, FAR) if stream == 0 else (FAR, NEAR)
    stages = [[(i, i ^ 1) for i in range(N_CTX)]]
    for turn in (0, 1):
        for step in order:
            pairs = []
            for i in range(N_CTX):
                y, x, c = place(i)
                if c == turn:
                    pairs.append((i, index_of(y, step[x], c)))
                else:
                    pairs.append((i, index_of(step[y], x, c)))
            stages.append(pairs)
    return stages


def chunk_place(me, owner, stream):
    my, mx, mc = me // 8, (me // 2) % 4, me % 2
    oy, ox, oc = place(owner)

    def bits(mine, theirs):
        g = mine ^ (mine >> 1)
        o = theirs ^ (theirs >> 1)
        same = 3 - (g ^ o)
        low, high = same & 1, same >> 1
        return (low, high) if stream == 0 else (high, low)

    xa, xb = bits(mx, ox)
    ya, yb = bits(my, oy)
    first, second = ((xa, xb), (ya, yb)) if oc == 0 else ((ya, yb), (xa, xb))
    same_core = 1 - (mc ^ oc)
    return same_core * 16 + first[0] * 8 + first[1] * 4 + second[0] * 2 + second[1]


def attend_kernel(heads, stream, last, *refs):
    place_ref, q_ref, do_ref, wk_ref, wv_ref, c4, c3, c2, c1, c0 = refs[:10]
    refs = refs[10:]
    if last:
        dcin_ref, refs = refs[0], refs[1:]
        out_ref, gq_ref, dw_ref, own_ref, p1_ref, p2_ref, p3_ref, p4_ref = refs[:8]
        refs = refs[8:]
    else:
        out_ref, gq_ref, dw_ref, dc_ref = refs[:4]
        refs = refs[4:]
    win, ct, absorbed, grad_lat, attended, grad_abs, grad_rope, acc = refs
    scale = QDIM ** -0.5

    win[0:64] = c4[...]
    for n, c in enumerate((c3, c2, c1, c0)):
        win[64 + 128 * n : 192 + 128 * n] = c[...]
    for half in range(2):
        ct[half] = win[half * HALF : half * HALF + SEEN].T

    for h in range(heads):
        q_n = q_ref[:, h * QDIM : h * QDIM + NOPE]
        q_r = q_ref[:, h * QDIM + NOPE : (h + 1) * QDIM]
        cols = slice(h * NOPE, (h + 1) * NOPE)
        a = dot(q_n, wk_ref[:, cols], 1, 1).astype(bf16)
        g = dot(do_ref[:, cols], wv_ref[:, cols], 1, 1).astype(bf16)
        for half in range(2):
            rows = slice(half * HALF, (half + 1) * HALF)
            to = slice(h * HALF, (h + 1) * HALF)
            absorbed[half, to, :LATENT] = a[rows]
            absorbed[half, to, LATENT:WIDE] = q_r[rows]
            grad_lat[half, to] = g[rows]

    if last:
        acc[...] = dcin_ref[...]
    else:
        acc[...] = jnp.zeros_like(acc)

    own = c0[:, WIDE:PACKED].astype(f32)
    query_ids = own[:, 0:1] * 128.0 + own[:, 1:2]
    for half in range(2):
        rows = slice(half * HALF, (half + 1) * HALF)
        keys = slice(half * HALF, half * HALF + SEEN)
        id_rows = ct[half, WIDE : WIDE + 16].astype(f32)
        key_ids = id_rows[0:1] * 128.0 + id_rows[1:2]
        j = lax.broadcasted_iota(jnp.int32, (HALF, SEEN), 1)
        t = lax.broadcasted_iota(jnp.int32, (HALF, SEEN), 0)
        visible = (key_ids == query_ids[rows]) & (j - BACK <= t)
        bias = jnp.where(visible, 0.0, HIDDEN)

        a = absorbed[half][:, :WIDE]
        g = grad_lat[half]
        s = dot(a, ct[half][:WIDE]).reshape(heads, HALF, SEEN) * scale + bias[None]
        s = jnp.exp(s - jnp.max(s, axis=-1, keepdims=True))
        p = s * (1.0 / jnp.sum(s, axis=-1, keepdims=True))
        p_bf = p.astype(bf16).reshape(heads * HALF, SEEN)
        dp = dot(g, ct[half][:LATENT]).reshape(heads, HALF, SEEN)
        delta = jnp.sum(p * dp, axis=-1, keepdims=True)
        ds = (p * (dp - delta) * scale).astype(bf16).reshape(heads * HALF, SEEN)
        att = dot(p_bf, win[keys, :LATENT]).astype(bf16)
        ga = dot(ds, win[keys, :WIDE])
        ga_bf = ga[:, :LATENT].astype(bf16)
        for h in range(heads):
            of = slice(h * HALF, (h + 1) * HALF)
            attended[h, rows] = att[of]
            grad_abs[h, rows] = ga_bf[of]
            grad_rope[h, rows] = ga[of, LATENT:WIDE]
        acc[keys, :LATENT] += dot(p_bf, g, 0, 0)
        acc[keys] += dot(ds, a, 0, 0)

    spots = [pl.multiple_of(place_ref[o] * CHUNK, CHUNK) for o in range(N_CTX)]
    for h in range(heads):
        cols = slice(h * NOPE, (h + 1) * NOPE)
        att = attended[h]
        ga = grad_abs[h]
        out_ref[:, cols] = dot(att, wv_ref[:, cols]).astype(bf16)
        gq_ref[:, h * QDIM : h * QDIM + NOPE] = dot(ga, wk_ref[:, cols])
        gq_ref[:, h * QDIM + NOPE : (h + 1) * QDIM] = grad_rope[h]
        dwk = dot(ga, q_ref[:, h * QDIM : h * QDIM + NOPE], 0, 0).astype(bf16)
        dwv = dot(att, do_ref[:, cols], 0, 0).astype(bf16)
        wv_cols = slice((heads + h) * NOPE, (heads + h + 1) * NOPE)
        for o in range(N_CTX):
            dw_ref[pl.ds(spots[o], CHUNK), cols] = dwk[o * CHUNK : (o + 1) * CHUNK]
            dw_ref[pl.ds(spots[o], CHUNK), wv_cols] = dwv[o * CHUNK : (o + 1) * CHUNK]

    if last:
        p4_ref[...] = acc[0:64].astype(bf16)
        p3_ref[...] = acc[64:192].astype(bf16)
        p2_ref[...] = acc[192:320].astype(bf16)
        p1_ref[...] = acc[320:448].astype(bf16)
        own_ref[...] = acc[448:576]
    else:
        dc_ref[...] = acc[...]


def attend(group, groups, heads, places, blocks, queries, out_grad, w_uk, w_uv, so_far):
    last = group == groups - 1
    whole = lambda shape: pl.BlockSpec(shape, lambda i: (0,) * len(shape))
    part = lambda rows, width: pl.BlockSpec((rows, width), lambda i: (0, group))
    in_specs = [
        pl.BlockSpec(memory_space=pltpu.SMEM),
        part(TOK, heads * QDIM),
        part(TOK, heads * NOPE),
        part(LATENT, heads * NOPE),
        part(LATENT, heads * NOPE),
        whole((HALF, PACKED)),
    ] + [whole((TOK, PACKED))] * 4
    args = [places, queries, out_grad, w_uk, w_uv] + blocks
    shapes = [
        jax.ShapeDtypeStruct((TOK, heads * NOPE), bf16),
        jax.ShapeDtypeStruct((TOK, heads * QDIM), f32),
        jax.ShapeDtypeStruct((LATENT, 2 * heads * NOPE), bf16),
    ]
    if last:
        in_specs.append(whole((WINDOW, WIDE)))
        args.append(so_far)
        shapes += [jax.ShapeDtypeStruct((TOK, WIDE), f32)]
        shapes += [jax.ShapeDtypeStruct((TOK, WIDE), bf16)] * 3
        shapes += [jax.ShapeDtypeStruct((HALF, WIDE), bf16)]
    else:
        shapes += [jax.ShapeDtypeStruct((WINDOW, WIDE), f32)]
    rows = heads * HALF
    return pl.pallas_call(
        functools.partial(attend_kernel, heads, group % 2, last),
        grid=(1,),
        in_specs=in_specs,
        out_specs=[whole(s.shape) for s in shapes],
        out_shape=shapes,
        scratch_shapes=[
            pltpu.VMEM((WINDOW, PACKED), bf16),
            pltpu.VMEM((2, PACKED, SEEN), bf16),
            pltpu.VMEM((2, rows, PACKED), bf16),
            pltpu.VMEM((2, rows, LATENT), bf16),
            pltpu.VMEM((heads, TOK, LATENT), bf16),
            pltpu.VMEM((heads, TOK, LATENT), bf16),
            pltpu.VMEM((heads, TOK, ROPE), f32),
            pltpu.VMEM((WINDOW, WIDE), f32),
        ],
        compiler_params=pltpu.CompilerParams(vmem_limit_bytes=52 * 2**20),
        cost_estimate=pl.CostEstimate(
            flops=int(2 * 2.1e9), bytes_accessed=8 * 2**20, transcendentals=rows * 2 * SEEN
        ),
    )(*args)


def passed_along(x, by):
    pairs = [(i, i + by) for i in range(N_CTX) if 0 <= i + by < N_CTX]
    return lax.ppermute(x, "ctx", pairs)


def halve(x, stream):
    stages = halving_pairs(stream)
    for n, pairs in enumerate(stages):
        h = x.shape[0] // 2
        got = lax.ppermute(x[:h], "ctx", pairs)
        x = x[h:].astype(f32) + got.astype(f32)
        if n < len(stages) - 1:
            x = x.astype(bf16)
    return x


def sum_over_head(x):
    me = lax.axis_index("head")
    odd = (me & 1) == 1
    low, high = x[:HALF], x[HALF:]
    swap = lambda y, d: lax.ppermute(y, "head", [(i, i ^ d) for i in range(8)])
    got = swap(jnp.where(odd, low, high).astype(bf16), 1)
    mine = jnp.where(odd, high, low) + got.astype(f32)
    for d in (2, 4):
        mine = mine.astype(bf16)
        mine = mine.astype(f32) + swap(mine, d).astype(f32)
    mine = mine.astype(bf16)
    other = swap(mine, 1)
    mine, other = mine.astype(f32), other.astype(f32)
    return jnp.concatenate([jnp.where(odd, other, mine), jnp.where(odd, mine, other)], axis=0)


def body(queries, latents, w_uk, w_uv, out_grad, doc_ids):
    ctx = lax.axis_index("ctx")
    groups, heads = 2, 8
    number = doc_ids + 1
    packed = jnp.concatenate(
        [
            latents,
            (number // 128).astype(bf16)[:, None],
            (number % 128).astype(bf16)[:, None],
            jnp.zeros((TOK, PACKED - WIDE - 2), bf16),
        ],
        axis=1,
    )
    blocks = [passed_along(packed[HALF:], 4)]
    blocks += [passed_along(packed, d) for d in (3, 2, 1)] + [packed]
    outs, gqs, weights = [], [], []
    so_far = None
    for group in range(groups):
        places = jnp.stack([chunk_place(ctx, o, group % 2) for o in range(N_CTX)]).astype(jnp.int32)
        res = attend(group, groups, heads, places, blocks, queries, out_grad, w_uk, w_uv, so_far)
        outs.append(res[0])
        gqs.append(res[1])
        weights.append(halve(res[2], group % 2))
        so_far = res[3]
    total, p1, p2, p3, p4 = res[3:]
    for d, piece in ((1, p1), (2, p2), (3, p3)):
        total = total + passed_along(piece, -d).astype(f32)
    far = passed_along(p4, -4).astype(f32)
    total = total + jnp.concatenate([jnp.zeros_like(far), far], axis=0)
    total = sum_over_head(total)
    cut = heads * NOPE
    return (
        jnp.concatenate(outs, axis=1),
        jnp.concatenate(gqs, axis=1),
        total,
        jnp.concatenate([w[:, :cut] for w in weights], axis=1),
        jnp.concatenate([w[:, cut:] for w in weights], axis=1),
    )


def solution(mesh):
    placed = (
        P("ctx", "head"),
        P("ctx", None),
        P(None, "head"),
        P(None, "head"),
        P("ctx", "head"),
        P("ctx"),
    )
    return jax.shard_map(
        body,
        mesh=mesh,
        in_specs=placed,
        out_specs=(
            P("ctx", "head"),
            P("ctx", "head"),
            P("ctx", None),
            P("ctx", "head"),
            P("ctx", "head"),
        ),
        check_vma=False,
    )
```

```python
import functools

import jax
import jax.numpy as jnp
from jax import lax
from jax.experimental import pallas as pl
from jax.experimental.pallas import tpu as pltpu
from jax.sharding import PartitionSpec as P

LATENT = 512
ROPE = 64
NOPE = 128
WIDE = LATENT + ROPE
QDIM = NOPE + ROPE
SPAN = 4
TOK = 128
HALF = 64
BACK = 448
WINDOW = BACK + TOK
SEEN = BACK + HALF
PACKED = 640
N_CTX = 32
CHUNK = LATENT // N_CTX
HIDDEN = -1e30

bf16 = jnp.bfloat16
f32 = jnp.float32


def dot(a, b, ca=1, cb=0):
    return lax.dot_general(a, b, (((ca,), (cb,)), ((), ())), preferred_element_type=f32)


def place(i):
    return i // 8, (i // 2) % 4, i % 2


def index_of(y, x, c):
    return (y * 4 + x) * 2 + c


NEAR = {0: 1, 1: 0, 2: 3, 3: 2}
FAR = {0: 3, 3: 0, 1: 2, 2: 1}


def halving_pairs(stream):
    order = (NEAR, FAR) if stream == 0 else (FAR, NEAR)
    stages = []
    for turn, steps in ((0, order), (1, (NEAR, FAR))):
        for step in steps:
            pairs = []
            for i in range(N_CTX):
                y, x, c = place(i)
                if c == turn:
                    pairs.append((i, index_of(y, step[x], c)))
                else:
                    pairs.append((i, index_of(step[y], x, c)))
            stages.append(pairs)
    return stages


def chunk_places(me, stream):
    chips = jnp.arange(16, dtype=jnp.int32)
    my, mx, mc = me // 8, (me // 2) % 4, me % 2

    def bits(mine, theirs):
        same = 3 - ((mine ^ (mine >> 1)) ^ (theirs ^ (theirs >> 1)))
        return same & 1, same >> 1

    (xl, xh), (yl, yh) = bits(mx, chips % 4), bits(my, chips // 4)
    if stream == 0:
        x_first = xl * 8 + xh * 4 + yl * 2 + yh
        y_first = yl * 8 + yh * 4 + xl * 2 + xh
    else:
        x_first = xh * 8 + xl * 4 + yl * 2 + yh
        y_first = yh * 8 + yl * 4 + xl * 2 + xh
    keep = jnp.where(mc == 0, x_first, y_first)
    send = jnp.where(mc == 0, y_first, x_first)
    return [keep, send]


def attend_kernel(heads, *refs):
    place_ref, q_ref, do_ref, wk_ref, wv_ref, c4, c3, c2, c1, c0 = refs[:10]
    out_ref, gq_ref, send_ref, keep_ref, own_ref, p1_ref, p2_ref, p3_ref, p4_ref = refs[10:19]
    win, ct, absorbed, grad_lat, attended, grad_abs, grad_rope, acc = refs[19:]
    step = pl.program_id(0)
    scale = QDIM ** -0.5

    @pl.when(step == 0)
    def _():
        win[0:64] = c4[...]
        for n, c in enumerate((c3, c2, c1, c0)):
            win[64 + 128 * n : 192 + 128 * n] = c[...]
        for half in range(2):
            ct[half] = win[half * HALF : half * HALF + SEEN].T
        acc[...] = jnp.zeros_like(acc)

    for h in range(heads):
        q_n = q_ref[:, h * QDIM : h * QDIM + NOPE]
        q_r = q_ref[:, h * QDIM + NOPE : (h + 1) * QDIM]
        cols = slice(h * NOPE, (h + 1) * NOPE)
        a = dot(q_n, wk_ref[:, cols], 1, 1).astype(bf16)
        g = dot(do_ref[:, cols], wv_ref[:, cols], 1, 1).astype(bf16)
        for half in range(2):
            rows = slice(half * HALF, (half + 1) * HALF)
            to = slice(h * HALF, (h + 1) * HALF)
            absorbed[half, to, :LATENT] = a[rows]
            absorbed[half, to, LATENT:WIDE] = q_r[rows]
            grad_lat[half, to] = g[rows]

    own = c0[:, WIDE:PACKED].astype(f32)
    query_ids = own[:, 0:1] * 128.0 + own[:, 1:2]
    for half in range(2):
        rows = slice(half * HALF, (half + 1) * HALF)
        keys = slice(half * HALF, half * HALF + SEEN)
        id_rows = ct[half, WIDE : WIDE + 16].astype(f32)
        key_ids = id_rows[0:1] * 128.0 + id_rows[1:2]
        j = lax.broadcasted_iota(jnp.int32, (HALF, SEEN), 1)
        t = lax.broadcasted_iota(jnp.int32, (HALF, SEEN), 0)
        visible = (key_ids == query_ids[rows]) & (j - BACK <= t)
        bias = jnp.where(visible, 0.0, HIDDEN)

        a = absorbed[half][:, :WIDE]
        g = grad_lat[half]
        s = dot(a, ct[half][:WIDE]).reshape(heads, HALF, SEEN) * scale + bias[None]
        s = jnp.exp(s - jnp.max(s, axis=-1, keepdims=True))
        p = s * (1.0 / jnp.sum(s, axis=-1, keepdims=True))
        p_bf = p.astype(bf16).reshape(heads * HALF, SEEN)
        dp = dot(g, ct[half][:LATENT]).reshape(heads, HALF, SEEN)
        delta = jnp.sum(p * dp, axis=-1, keepdims=True)
        ds = (p * (dp - delta) * scale).astype(bf16).reshape(heads * HALF, SEEN)
        att = dot(p_bf, win[keys, :LATENT]).astype(bf16)
        ga = dot(ds, win[keys, :WIDE])
        ga_bf = ga[:, :LATENT].astype(bf16)
        for h in range(heads):
            of = slice(h * HALF, (h + 1) * HALF)
            attended[h, rows] = att[of]
            grad_abs[h, rows] = ga_bf[of]
            grad_rope[h, rows] = ga[of, LATENT:WIDE]
        acc[keys, :LATENT] += dot(p_bf, g, 0, 0)
        acc[keys] += dot(ds, a, 0, 0)

    core = place_ref[64]
    spots = [pl.multiple_of(place_ref[n] * CHUNK, CHUNK) for n in range(64)]
    for h in range(heads):
        cols = slice(h * NOPE, (h + 1) * NOPE)
        out_ref[:, cols] = dot(attended[h], wv_ref[:, cols]).astype(bf16)
        gq_ref[:, h * QDIM : h * QDIM + NOPE] = dot(grad_abs[h], wk_ref[:, cols])
        gq_ref[:, h * QDIM + NOPE : (h + 1) * QDIM] = grad_rope[h]
        dwk = dot(grad_abs[h], q_ref[:, h * QDIM : h * QDIM + NOPE], 0, 0).astype(bf16)
        dwv = dot(attended[h], do_ref[:, cols], 0, 0).astype(bf16)
        for m, dw in enumerate((dwk, dwv)):
            for n in range(16):
                zero = dw[2 * n * CHUNK : (2 * n + 1) * CHUNK]
                one = dw[(2 * n + 1) * CHUNK : (2 * n + 2) * CHUNK]
                keep, send = spots[32 * m + n], spots[32 * m + 16 + n]
                keep_ref[m, pl.ds(keep, CHUNK), cols] = jnp.where(core == 0, zero, one)
                send_ref[m, pl.ds(send, CHUNK), cols] = jnp.where(core == 0, one, zero)

    @pl.when(step == pl.num_programs(0) - 1)
    def _():
        p4_ref[...] = acc[0:64].astype(bf16)
        p3_ref[...] = acc[64:192].astype(bf16)
        p2_ref[...] = acc[192:320].astype(bf16)
        p1_ref[...] = acc[320:448].astype(bf16)
        own_ref[...] = acc[448:576]


def whole(shape):
    return pl.BlockSpec(shape, lambda i: (0,) * len(shape))


def part(rows, width):
    return pl.BlockSpec((rows, width), lambda i: (0, i))


def attend(steps, heads, places, blocks, queries, out_grad, w_uk, w_uv):
    all_heads = steps * heads
    rows = heads * HALF
    shapes = [
        jax.ShapeDtypeStruct((TOK, all_heads * NOPE), bf16),
        jax.ShapeDtypeStruct((TOK, all_heads * QDIM), f32),
        jax.ShapeDtypeStruct((2, LATENT // 2, all_heads * NOPE), bf16),
        jax.ShapeDtypeStruct((2, LATENT // 2, all_heads * NOPE), bf16),
        jax.ShapeDtypeStruct((TOK, WIDE), f32),
    ]
    shapes += [jax.ShapeDtypeStruct((TOK, WIDE), bf16)] * 3
    shapes += [jax.ShapeDtypeStruct((HALF, WIDE), bf16)]
    halves = pl.BlockSpec((2, LATENT // 2, heads * NOPE), lambda i: (0, 0, i))
    return pl.pallas_call(
        functools.partial(attend_kernel, heads),
        grid=(steps,),
        in_specs=[
            pl.BlockSpec(memory_space=pltpu.SMEM),
            part(TOK, heads * QDIM),
            part(TOK, heads * NOPE),
            part(LATENT, heads * NOPE),
            part(LATENT, heads * NOPE),
            whole((HALF, PACKED)),
        ]
        + [whole((TOK, PACKED))] * 4,
        out_specs=[part(TOK, heads * NOPE), part(TOK, heads * QDIM), halves, halves]
        + [whole(s.shape) for s in shapes[4:]],
        out_shape=shapes,
        scratch_shapes=[
            pltpu.VMEM((WINDOW, PACKED), bf16),
            pltpu.VMEM((2, PACKED, SEEN), bf16),
            pltpu.VMEM((2, rows, PACKED), bf16),
            pltpu.VMEM((2, rows, LATENT), bf16),
            pltpu.VMEM((heads, TOK, LATENT), bf16),
            pltpu.VMEM((heads, TOK, LATENT), bf16),
            pltpu.VMEM((heads, TOK, ROPE), f32),
            pltpu.VMEM((WINDOW, WIDE), f32),
        ],
        compiler_params=pltpu.CompilerParams(vmem_limit_bytes=54 * 2**20),
        cost_estimate=pl.CostEstimate(
            flops=int(18e9), bytes_accessed=16 * 2**20, transcendentals=2 * steps * rows * SEEN
        ),
    )(places, queries, out_grad, w_uk, w_uv, *blocks)


def passed_along(x, by):
    pairs = [(i, i + by) for i in range(N_CTX) if 0 <= i + by < N_CTX]
    return lax.ppermute(x, "ctx", pairs)


def over_core(send, keep):
    got = lax.ppermute(send, "ctx", [(i, i ^ 1) for i in range(N_CTX)])
    return (keep.astype(f32) + got.astype(f32)).astype(bf16)


def halved(x, pairs):
    h = x.shape[1] // 2
    got = lax.ppermute(x[:, :h], "ctx", pairs)
    return x[:, h:].astype(f32) + got.astype(f32)


def sum_over_head(x):
    me = lax.axis_index("head")
    odd = (me & 1) == 1
    low, high = x[:HALF], x[HALF:]
    swap = lambda y, d: lax.ppermute(y, "head", [(i, i ^ d) for i in range(8)])
    got = swap(jnp.where(odd, low, high).astype(bf16), 1)
    mine = jnp.where(odd, high, low) + got.astype(f32)
    for d in (2, 6):
        mine = mine.astype(bf16)
        mine = mine.astype(f32) + swap(mine, d).astype(f32)
    mine = mine.astype(bf16)
    other = swap(mine, 1)
    mine, other = mine.astype(f32), other.astype(f32)
    return jnp.concatenate([jnp.where(odd, other, mine), jnp.where(odd, mine, other)], axis=0)


def body(queries, latents, w_uk, w_uv, out_grad, doc_ids):
    ctx = lax.axis_index("ctx")
    number = doc_ids + 1
    packed = jnp.concatenate(
        [
            latents,
            (number // 128).astype(bf16)[:, None],
            (number % 128).astype(bf16)[:, None],
            jnp.zeros((TOK, PACKED - WIDE - 2), bf16),
        ],
        axis=1,
    )
    blocks = [passed_along(packed[HALF:], 4)]
    blocks += [passed_along(packed, d) for d in (3, 2, 1)] + [packed]
    places = chunk_places(ctx, 0) + chunk_places(ctx, 1) + [(ctx % 2)[None]]
    places = jnp.concatenate(places).astype(jnp.int32)
    res = attend(2, 8, places, blocks, queries, out_grad, w_uk, w_uv)
    outs, gq, send, keep, total, p1, p2, p3, p4 = res
    pieces = [passed_along(piece, -d) for d, piece in ((1, p1), (2, p2), (3, p3), (4, p4))]
    terms = over_core(send, keep)
    terms = [terms[:1], terms[1:]]
    stages = [halving_pairs(stream) for stream in range(2)]
    for n in range(2):
        terms = [halved(x, stages[g][n]).astype(bf16) for g, x in enumerate(terms)]
    for piece in pieces[:3]:
        total = total + piece.astype(f32)
    far = pieces[3].astype(f32)
    total = total + jnp.concatenate([jnp.zeros_like(far), far], axis=0)
    total = sum_over_head(total)
    x = jnp.concatenate(terms, axis=0)
    x = halved(x, stages[0][2]).astype(bf16)
    x = halved(x, stages[0][3])
    return outs, gq, total, x[0], x[1]


def solution(mesh):
    placed = (
        P("ctx", "head"),
        P("ctx", None),
        P(None, "head"),
        P(None, "head"),
        P("ctx", "head"),
        P("ctx"),
    )
    return jax.shard_map(
        body,
        mesh=mesh,
        in_specs=placed,
        out_specs=(
            P("ctx", "head"),
            P("ctx", "head"),
            P("ctx", None),
            P("ctx", "head"),
            P("ctx", "head"),
        ),
        check_vma=False,
    )
```

```python
import functools

import jax
import jax.numpy as jnp
from jax import lax
from jax.experimental import pallas as pl
from jax.experimental.pallas import tpu as pltpu
from jax.sharding import PartitionSpec as P

LATENT = 512
ROPE = 64
NOPE = 128
WIDE = LATENT + ROPE
QDIM = NOPE + ROPE
SPAN = 4
TOK = 128
HALF = 64
BACK = 448
WINDOW = BACK + TOK
SEEN = BACK + HALF
PACKED = 640
N_CTX = 32
CHUNK = LATENT // N_CTX
HIDDEN = -1e30

bf16 = jnp.bfloat16
f32 = jnp.float32


def dot(a, b, ca=1, cb=0):
    return lax.dot_general(a, b, (((ca,), (cb,)), ((), ())), preferred_element_type=f32)


def place(i):
    return i // 8, (i // 2) % 4, i % 2


def index_of(y, x, c):
    return (y * 4 + x) * 2 + c


NEAR = {0: 1, 1: 0, 2: 3, 3: 2}
FAR = {0: 3, 3: 0, 1: 2, 2: 1}


OPPOSITE = {0: 2, 2: 0, 1: 3, 3: 1}


def ring_pairs(turn, step):
    pairs = []
    for i in range(N_CTX):
        y, x, c = place(i)
        pairs.append((i, index_of(y, step[x], c) if c == turn else index_of(step[y], x, c)))
    return pairs


def chunk_places(me):
    chips = jnp.arange(16, dtype=jnp.int32)
    my, mx, mc = me // 8, (me // 2) % 4, me % 2

    def bits(mine, theirs):
        same = 3 - ((mine ^ (mine >> 1)) ^ (theirs ^ (theirs >> 1)))
        return same & 1, same >> 1

    (xl, xh), (yl, yh) = bits(mx, chips % 4), bits(my, chips // 4)
    x_first = xl * 8 + xh * 4 + yl * 2 + yh
    y_first = yl * 8 + yh * 4 + xl * 2 + xh
    keep = jnp.where(mc == 0, x_first, y_first)
    send = jnp.where(mc == 0, y_first, x_first)
    return [keep, send]


def attend_kernel(heads, *refs):
    place_ref, q_ref, do_ref, wk_ref, wv_ref, c4, c3, c2, c1, c0 = refs[:10]
    out_ref, gq_ref, send_ref, keep_ref, own_ref, p1_ref, p2_ref, p3_ref, p4_ref = refs[10:19]
    win, ct, absorbed, grad_lat, attended, grad_abs, grad_rope, acc = refs[19:]
    step = pl.program_id(0)
    scale = QDIM ** -0.5

    @pl.when(step == 0)
    def _():
        win[0:64] = c4[...]
        for n, c in enumerate((c3, c2, c1, c0)):
            win[64 + 128 * n : 192 + 128 * n] = c[...]
        for half in range(2):
            ct[half] = win[half * HALF : half * HALF + SEEN].T
        acc[...] = jnp.zeros_like(acc)

    for h in range(heads):
        q_n = q_ref[:, h * QDIM : h * QDIM + NOPE]
        q_r = q_ref[:, h * QDIM + NOPE : (h + 1) * QDIM]
        cols = slice(h * NOPE, (h + 1) * NOPE)
        a = dot(q_n, wk_ref[:, cols], 1, 1).astype(bf16)
        g = dot(do_ref[:, cols], wv_ref[:, cols], 1, 1).astype(bf16)
        for half in range(2):
            rows = slice(half * HALF, (half + 1) * HALF)
            to = slice(h * HALF, (h + 1) * HALF)
            absorbed[half, to, :LATENT] = a[rows]
            absorbed[half, to, LATENT:WIDE] = q_r[rows]
            grad_lat[half, to] = g[rows]

    own = c0[:, WIDE:PACKED].astype(f32)
    query_ids = own[:, 0:1] * 128.0 + own[:, 1:2]
    for half in range(2):
        rows = slice(half * HALF, (half + 1) * HALF)
        keys = slice(half * HALF, half * HALF + SEEN)
        id_rows = ct[half, WIDE : WIDE + 16].astype(f32)
        key_ids = id_rows[0:1] * 128.0 + id_rows[1:2]
        j = lax.broadcasted_iota(jnp.int32, (HALF, SEEN), 1)
        t = lax.broadcasted_iota(jnp.int32, (HALF, SEEN), 0)
        visible = (key_ids == query_ids[rows]) & (j - BACK <= t)
        bias = jnp.where(visible, 0.0, HIDDEN)

        a = absorbed[half][:, :WIDE]
        g = grad_lat[half]
        s = dot(a, ct[half][:WIDE]).reshape(heads, HALF, SEEN) * scale + bias[None]
        s = jnp.exp(s - jnp.max(s, axis=-1, keepdims=True))
        p = s * (1.0 / jnp.sum(s, axis=-1, keepdims=True))
        p_bf = p.astype(bf16).reshape(heads * HALF, SEEN)
        dp = dot(g, ct[half][:LATENT]).reshape(heads, HALF, SEEN)
        delta = jnp.sum(p * dp, axis=-1, keepdims=True)
        ds = (p * (dp - delta) * scale).astype(bf16).reshape(heads * HALF, SEEN)
        att = dot(p_bf, win[keys, :LATENT]).astype(bf16)
        ga = dot(ds, win[keys, :WIDE])
        ga_bf = ga[:, :LATENT].astype(bf16)
        for h in range(heads):
            of = slice(h * HALF, (h + 1) * HALF)
            attended[h, rows] = att[of]
            grad_abs[h, rows] = ga_bf[of]
            grad_rope[h, rows] = ga[of, LATENT:WIDE]
        acc[keys, :LATENT] += dot(p_bf, g, 0, 0)
        acc[keys] += dot(ds, a, 0, 0)

    core = place_ref[64]
    spots = [pl.multiple_of(place_ref[n] * CHUNK, CHUNK) for n in range(64)]
    for h in range(heads):
        cols = slice(h * NOPE, (h + 1) * NOPE)
        out_ref[:, cols] = dot(attended[h], wv_ref[:, cols]).astype(bf16)
        gq_ref[:, h * QDIM : h * QDIM + NOPE] = dot(grad_abs[h], wk_ref[:, cols])
        gq_ref[:, h * QDIM + NOPE : (h + 1) * QDIM] = grad_rope[h]
        dwk = dot(grad_abs[h], q_ref[:, h * QDIM : h * QDIM + NOPE], 0, 0).astype(bf16)
        dwv = dot(attended[h], do_ref[:, cols], 0, 0).astype(bf16)
        for m, dw in enumerate((dwk, dwv)):
            for n in range(16):
                zero = dw[2 * n * CHUNK : (2 * n + 1) * CHUNK]
                one = dw[(2 * n + 1) * CHUNK : (2 * n + 2) * CHUNK]
                keep, send = spots[32 * m + n], spots[32 * m + 16 + n]
                keep_ref[m, pl.ds(keep, CHUNK), cols] = jnp.where(core == 0, zero, one)
                send_ref[m, pl.ds(send, CHUNK), cols] = jnp.where(core == 0, one, zero)

    @pl.when(step == pl.num_programs(0) - 1)
    def _():
        p4_ref[...] = acc[0:64].astype(bf16)
        p3_ref[...] = acc[64:192].astype(bf16)
        p2_ref[...] = acc[192:320].astype(bf16)
        p1_ref[...] = acc[320:448].astype(bf16)
        own_ref[...] = acc[448:576]


def whole(shape):
    return pl.BlockSpec(shape, lambda i: (0,) * len(shape))


def part(rows, width):
    return pl.BlockSpec((rows, width), lambda i: (0, i))


def attend(steps, heads, places, blocks, queries, out_grad, w_uk, w_uv):
    all_heads = steps * heads
    rows = heads * HALF
    shapes = [
        jax.ShapeDtypeStruct((TOK, all_heads * NOPE), bf16),
        jax.ShapeDtypeStruct((TOK, all_heads * QDIM), f32),
        jax.ShapeDtypeStruct((2, LATENT // 2, all_heads * NOPE), bf16),
        jax.ShapeDtypeStruct((2, LATENT // 2, all_heads * NOPE), bf16),
        jax.ShapeDtypeStruct((TOK, WIDE), f32),
    ]
    shapes += [jax.ShapeDtypeStruct((TOK, WIDE), bf16)] * 3
    shapes += [jax.ShapeDtypeStruct((HALF, WIDE), bf16)]
    halves = pl.BlockSpec((2, LATENT // 2, heads * NOPE), lambda i: (0, 0, i))
    return pl.pallas_call(
        functools.partial(attend_kernel, heads),
        grid=(steps,),
        in_specs=[
            pl.BlockSpec(memory_space=pltpu.SMEM),
            part(TOK, heads * QDIM),
            part(TOK, heads * NOPE),
            part(LATENT, heads * NOPE),
            part(LATENT, heads * NOPE),
            whole((HALF, PACKED)),
        ]
        + [whole((TOK, PACKED))] * 4,
        out_specs=[part(TOK, heads * NOPE), part(TOK, heads * QDIM), halves, halves]
        + [whole(s.shape) for s in shapes[4:]],
        out_shape=shapes,
        scratch_shapes=[
            pltpu.VMEM((WINDOW, PACKED), bf16),
            pltpu.VMEM((2, PACKED, SEEN), bf16),
            pltpu.VMEM((2, rows, PACKED), bf16),
            pltpu.VMEM((2, rows, LATENT), bf16),
            pltpu.VMEM((heads, TOK, LATENT), bf16),
            pltpu.VMEM((heads, TOK, LATENT), bf16),
            pltpu.VMEM((heads, TOK, ROPE), f32),
            pltpu.VMEM((WINDOW, WIDE), f32),
        ],
        compiler_params=pltpu.CompilerParams(vmem_limit_bytes=54 * 2**20),
        cost_estimate=pl.CostEstimate(
            flops=int(18e9), bytes_accessed=16 * 2**20, transcendentals=2 * steps * rows * SEEN
        ),
    )(places, queries, out_grad, w_uk, w_uv, *blocks)


def passed_along(x, by):
    pairs = [(i, i + by) for i in range(N_CTX) if 0 <= i + by < N_CTX]
    return lax.ppermute(x, "ctx", pairs)


def over_core(send, keep):
    got = lax.ppermute(send, "ctx", [(i, i ^ 1) for i in range(N_CTX)])
    return (keep.astype(f32) + got.astype(f32)).astype(bf16)


def over_ring(x, turn):
    q = x.shape[1] // 4
    gots = [
        lax.ppermute(x[:, n * q : (n + 1) * q], "ctx", ring_pairs(turn, step))
        for n, step in enumerate((OPPOSITE, NEAR, FAR))
    ]
    return x[:, 3 * q :], gots


def sum_over_head(x):
    me = lax.axis_index("head")
    odd = (me & 1) == 1
    low, high = x[:HALF], x[HALF:]
    swap = lambda y, d: lax.ppermute(y, "head", [(i, i ^ d) for i in range(8)])
    got = swap(jnp.where(odd, low, high).astype(bf16), 1)
    mine = jnp.where(odd, high, low) + got.astype(f32)
    for d in (2, 6):
        mine = mine.astype(bf16)
        mine = mine.astype(f32) + swap(mine, d).astype(f32)
    mine = mine.astype(bf16)
    other = swap(mine, 1)
    mine, other = mine.astype(f32), other.astype(f32)
    return jnp.concatenate([jnp.where(odd, other, mine), jnp.where(odd, mine, other)], axis=0)


def body(queries, latents, w_uk, w_uv, out_grad, doc_ids):
    ctx = lax.axis_index("ctx")
    number = doc_ids + 1
    packed = jnp.concatenate(
        [
            latents,
            (number // 128).astype(bf16)[:, None],
            (number % 128).astype(bf16)[:, None],
            jnp.zeros((TOK, PACKED - WIDE - 2), bf16),
        ],
        axis=1,
    )
    blocks = [passed_along(packed[HALF:], 4)]
    blocks += [passed_along(packed, d) for d in (3, 2, 1)] + [packed]
    places = chunk_places(ctx) + chunk_places(ctx) + [(ctx % 2)[None]]
    places = jnp.concatenate(places).astype(jnp.int32)
    res = attend(2, 8, places, blocks, queries, out_grad, w_uk, w_uv)
    outs, gq, send, keep, total, p1, p2, p3, p4 = res
    pieces = [passed_along(piece, -d) for d, piece in ((1, p1), (2, p2), (3, p3), (4, p4))]
    terms = over_core(send, keep)
    keep, gots = over_ring(terms, 0)
    terms = sum((g.astype(f32) for g in gots), keep.astype(f32)).astype(bf16)
    for piece in pieces[:3]:
        total = total + piece.astype(f32)
    far = pieces[3].astype(f32)
    total = total + jnp.concatenate([jnp.zeros_like(far), far], axis=0)
    total = sum_over_head(total)
    keep, gots = over_ring(terms, 1)
    w_uk_grad, w_uv_grad = (sum((g[m].astype(f32) for g in gots), keep[m].astype(f32)) for m in range(2))
    return outs, gq, total, w_uk_grad, w_uv_grad


def solution(mesh):
    placed = (
        P("ctx", "head"),
        P("ctx", None),
        P(None, "head"),
        P(None, "head"),
        P("ctx", "head"),
        P("ctx"),
    )
    return jax.shard_map(
        body,
        mesh=mesh,
        in_specs=placed,
        out_specs=(
            P("ctx", "head"),
            P("ctx", "head"),
            P("ctx", None),
            P("ctx", "head"),
            P("ctx", "head"),
        ),
        check_vma=False,
    )
```

```python
import functools

import jax
import jax.numpy as jnp
from jax import lax
from jax.experimental import pallas as pl
from jax.experimental.pallas import tpu as pltpu
from jax.sharding import PartitionSpec as P

LATENT = 512
ROPE = 64
NOPE = 128
WIDE = LATENT + ROPE
QDIM = NOPE + ROPE
SPAN = 4
TOK = 128
HALF = 64
BACK = 448
WINDOW = BACK + TOK
SEEN = BACK + HALF
PACKED = 640
N_CTX = 32
CHUNK = LATENT // N_CTX
HIDDEN = -1e30

bf16 = jnp.bfloat16
f32 = jnp.float32


def dot(a, b, ca=1, cb=0):
    return lax.dot_general(a, b, (((ca,), (cb,)), ((), ())), preferred_element_type=f32)


def place(i):
    return i // 8, (i // 2) % 4, i % 2


def index_of(y, x, c):
    return (y * 4 + x) * 2 + c


NEAR = {0: 1, 1: 0, 2: 3, 3: 2}
FAR = {0: 3, 3: 0, 1: 2, 2: 1}


OPPOSITE = {0: 2, 2: 0, 1: 3, 3: 1}


def ring_pairs(turn, step):
    pairs = []
    for i in range(N_CTX):
        y, x, c = place(i)
        pairs.append((i, index_of(y, step[x], c) if c == turn else index_of(step[y], x, c)))
    return pairs


def chunk_places(me):
    chips = jnp.arange(16, dtype=jnp.int32)
    my, mx, mc = me // 8, (me // 2) % 4, me % 2

    def bits(mine, theirs):
        same = 3 - ((mine ^ (mine >> 1)) ^ (theirs ^ (theirs >> 1)))
        return same & 1, same >> 1

    (xl, xh), (yl, yh) = bits(mx, chips % 4), bits(my, chips // 4)
    x_first = xl * 8 + xh * 4 + yl * 2 + yh
    y_first = yl * 8 + yh * 4 + xl * 2 + xh
    keep = jnp.where(mc == 0, x_first, y_first)
    send = jnp.where(mc == 0, y_first, x_first)
    return [keep, send]


def attend_kernel(heads, *refs):
    place_ref, q_ref, do_ref, wk_ref, wv_ref, c4, c3, c2, c1, c0 = refs[:10]
    out_ref, gq_ref, send_ref, keep_ref, own_ref, p1_ref, p2_ref, p3_ref, p4_ref = refs[10:19]
    win, ct, absorbed, grad_lat, attended, grad_abs, grad_rope, acc = refs[19:]
    step = pl.program_id(0)
    scale = QDIM ** -0.5

    @pl.when(step == 0)
    def _():
        win[0:64] = c4[...]
        for n, c in enumerate((c3, c2, c1, c0)):
            win[64 + 128 * n : 192 + 128 * n] = c[...]
        for half in range(2):
            ct[half] = win[half * HALF : half * HALF + SEEN].T
        acc[...] = jnp.zeros_like(acc)

    for h in range(heads):
        q_n = q_ref[:, h * QDIM : h * QDIM + NOPE]
        q_r = q_ref[:, h * QDIM + NOPE : (h + 1) * QDIM]
        cols = slice(h * NOPE, (h + 1) * NOPE)
        a = dot(q_n, wk_ref[:, cols], 1, 1).astype(bf16)
        g = dot(do_ref[:, cols], wv_ref[:, cols], 1, 1).astype(bf16)
        for half in range(2):
            rows = slice(half * HALF, (half + 1) * HALF)
            to = slice(h * HALF, (h + 1) * HALF)
            absorbed[half, to, :LATENT] = a[rows]
            absorbed[half, to, LATENT:WIDE] = q_r[rows]
            grad_lat[half, to] = g[rows]

    own = c0[:, WIDE:PACKED].astype(f32)
    query_ids = own[:, 0:1] * 128.0 + own[:, 1:2]
    for half in range(2):
        rows = slice(half * HALF, (half + 1) * HALF)
        keys = slice(half * HALF, half * HALF + SEEN)
        id_rows = ct[half, WIDE : WIDE + 16].astype(f32)
        key_ids = id_rows[0:1] * 128.0 + id_rows[1:2]
        j = lax.broadcasted_iota(jnp.int32, (HALF, SEEN), 1)
        t = lax.broadcasted_iota(jnp.int32, (HALF, SEEN), 0)
        visible = (key_ids == query_ids[rows]) & (j - BACK <= t)
        bias = jnp.where(visible, 0.0, HIDDEN)

        a = absorbed[half][:, :WIDE]
        g = grad_lat[half]
        s = dot(a, ct[half][:WIDE]).reshape(heads, HALF, SEEN) * scale + bias[None]
        s = jnp.exp(s - jnp.max(s, axis=-1, keepdims=True))
        p = s * (1.0 / jnp.sum(s, axis=-1, keepdims=True))
        p_bf = p.astype(bf16).reshape(heads * HALF, SEEN)
        dp = dot(g, ct[half][:LATENT]).reshape(heads, HALF, SEEN)
        delta = jnp.sum(p * dp, axis=-1, keepdims=True)
        ds = (p * (dp - delta) * scale).astype(bf16).reshape(heads * HALF, SEEN)
        att = dot(p_bf, win[keys, :LATENT]).astype(bf16)
        ga = dot(ds, win[keys, :WIDE])
        ga_bf = ga[:, :LATENT].astype(bf16)
        for h in range(heads):
            of = slice(h * HALF, (h + 1) * HALF)
            attended[h, rows] = att[of]
            grad_abs[h, rows] = ga_bf[of]
            grad_rope[h, rows] = ga[of, LATENT:WIDE]
        acc[keys, :LATENT] += dot(p_bf, g, 0, 0)
        acc[keys] += dot(ds, a, 0, 0)

    core = place_ref[64]
    spots = [pl.multiple_of(place_ref[n] * CHUNK, CHUNK) for n in range(64)]
    for h in range(heads):
        cols = slice(h * NOPE, (h + 1) * NOPE)
        out_ref[:, cols] = dot(attended[h], wv_ref[:, cols]).astype(bf16)
        gq_ref[:, h * QDIM : h * QDIM + NOPE] = dot(grad_abs[h], wk_ref[:, cols])
        gq_ref[:, h * QDIM + NOPE : (h + 1) * QDIM] = grad_rope[h]
        dwk = dot(grad_abs[h], q_ref[:, h * QDIM : h * QDIM + NOPE], 0, 0).astype(bf16)
        dwv = dot(attended[h], do_ref[:, cols], 0, 0).astype(bf16)
        for m, dw in enumerate((dwk, dwv)):
            for n in range(16):
                zero = dw[2 * n * CHUNK : (2 * n + 1) * CHUNK]
                one = dw[(2 * n + 1) * CHUNK : (2 * n + 2) * CHUNK]
                keep, send = spots[32 * m + n], spots[32 * m + 16 + n]
                keep_ref[m, pl.ds(keep, CHUNK), cols] = jnp.where(core == 0, zero, one)
                send_ref[m, pl.ds(send, CHUNK), cols] = jnp.where(core == 0, one, zero)

    @pl.when(step == pl.num_programs(0) - 1)
    def _():
        p4_ref[...] = acc[0:64].astype(bf16)
        p3_ref[...] = acc[64:192].astype(bf16)
        p2_ref[...] = acc[192:320].astype(bf16)
        p1_ref[...] = acc[320:448].astype(bf16)
        own_ref[...] = acc[448:576]


def whole(shape):
    return pl.BlockSpec(shape, lambda i: (0,) * len(shape))


def part(rows, width):
    return pl.BlockSpec((rows, width), lambda i: (0, i))


def attend(steps, heads, places, blocks, queries, out_grad, w_uk, w_uv):
    all_heads = steps * heads
    rows = heads * HALF
    shapes = [
        jax.ShapeDtypeStruct((TOK, all_heads * NOPE), bf16),
        jax.ShapeDtypeStruct((TOK, all_heads * QDIM), f32),
        jax.ShapeDtypeStruct((2, LATENT // 2, all_heads * NOPE), bf16),
        jax.ShapeDtypeStruct((2, LATENT // 2, all_heads * NOPE), bf16),
        jax.ShapeDtypeStruct((TOK, WIDE), f32),
    ]
    shapes += [jax.ShapeDtypeStruct((TOK, WIDE), bf16)] * 3
    shapes += [jax.ShapeDtypeStruct((HALF, WIDE), bf16)]
    halves = pl.BlockSpec((2, LATENT // 2, heads * NOPE), lambda i: (0, 0, i))
    return pl.pallas_call(
        functools.partial(attend_kernel, heads),
        grid=(steps,),
        in_specs=[
            pl.BlockSpec(memory_space=pltpu.SMEM),
            part(TOK, heads * QDIM),
            part(TOK, heads * NOPE),
            part(LATENT, heads * NOPE),
            part(LATENT, heads * NOPE),
            whole((HALF, PACKED)),
        ]
        + [whole((TOK, PACKED))] * 4,
        out_specs=[part(TOK, heads * NOPE), part(TOK, heads * QDIM), halves, halves]
        + [whole(s.shape) for s in shapes[4:]],
        out_shape=shapes,
        scratch_shapes=[
            pltpu.VMEM((WINDOW, PACKED), bf16),
            pltpu.VMEM((2, PACKED, SEEN), bf16),
            pltpu.VMEM((2, rows, PACKED), bf16),
            pltpu.VMEM((2, rows, LATENT), bf16),
            pltpu.VMEM((heads, TOK, LATENT), bf16),
            pltpu.VMEM((heads, TOK, LATENT), bf16),
            pltpu.VMEM((heads, TOK, ROPE), f32),
            pltpu.VMEM((WINDOW, WIDE), f32),
        ],
        compiler_params=pltpu.CompilerParams(vmem_limit_bytes=40 * 2**20),
        cost_estimate=pl.CostEstimate(
            flops=int(18e9), bytes_accessed=16 * 2**20, transcendentals=2 * steps * rows * SEEN
        ),
    )(places, queries, out_grad, w_uk, w_uv, *blocks)


def passed_along(x, by):
    pairs = [(i, i + by) for i in range(N_CTX) if 0 <= i + by < N_CTX]
    return lax.ppermute(x, "ctx", pairs)


def over_core(send, keep):
    got = lax.ppermute(send, "ctx", [(i, i ^ 1) for i in range(N_CTX)])
    return (keep.astype(f32) + got.astype(f32)).astype(bf16)


def over_ring(x, turn):
    q = x.shape[1] // 4
    gots = [
        lax.ppermute(x[:, n * q : (n + 1) * q], "ctx", ring_pairs(turn, step))
        for n, step in enumerate((OPPOSITE, NEAR, FAR))
    ]
    return x[:, 3 * q :], gots


def sum_over_head(x):
    me = lax.axis_index("head")
    odd = (me & 1) == 1
    low, high = x[:HALF], x[HALF:]
    swap = lambda y, d: lax.ppermute(y, "head", [(i, i ^ d) for i in range(8)])
    got = swap(jnp.where(odd, low, high).astype(bf16), 1)
    mine = jnp.where(odd, high, low) + got.astype(f32)
    for d in (2, 6):
        mine = mine.astype(bf16)
        mine = mine.astype(f32) + swap(mine, d).astype(f32)
    mine = mine.astype(bf16)
    other = swap(mine, 1)
    mine, other = mine.astype(f32), other.astype(f32)
    return jnp.concatenate([jnp.where(odd, other, mine), jnp.where(odd, mine, other)], axis=0)


def body(queries, latents, w_uk, w_uv, out_grad, doc_ids):
    ctx = lax.axis_index("ctx")
    number = doc_ids + 1
    packed = jnp.concatenate(
        [
            latents,
            (number // 128).astype(bf16)[:, None],
            (number % 128).astype(bf16)[:, None],
            jnp.zeros((TOK, PACKED - WIDE - 2), bf16),
        ],
        axis=1,
    )
    blocks = [passed_along(packed[HALF:], 4)]
    blocks += [passed_along(packed, d) for d in (3, 2, 1)] + [packed]
    places = chunk_places(ctx) + chunk_places(ctx) + [(ctx % 2)[None]]
    places = jnp.concatenate(places).astype(jnp.int32)
    res = attend(2, 8, places, blocks, queries, out_grad, w_uk, w_uv)
    outs, gq, send, keep, total, p1, p2, p3, p4 = res
    pieces = [passed_along(piece, -d) for d, piece in ((1, p1), (2, p2), (3, p3), (4, p4))]
    terms = over_core(send, keep)
    keep, gots = over_ring(terms, 0)
    terms = sum((g.astype(f32) for g in gots), keep.astype(f32)).astype(bf16)
    for piece in pieces[:3]:
        total = total + piece.astype(f32)
    far = pieces[3].astype(f32)
    total = total + jnp.concatenate([jnp.zeros_like(far), far], axis=0)
    total = sum_over_head(total)
    keep, gots = over_ring(terms, 1)
    w_uk_grad, w_uv_grad = (sum((g[m].astype(f32) for g in gots), keep[m].astype(f32)) for m in range(2))
    return outs, gq, total, w_uk_grad, w_uv_grad


def solution(mesh):
    placed = (
        P("ctx", "head"),
        P("ctx", None),
        P(None, "head"),
        P(None, "head"),
        P("ctx", "head"),
        P("ctx"),
    )
    return jax.shard_map(
        body,
        mesh=mesh,
        in_specs=placed,
        out_specs=(
            P("ctx", "head"),
            P("ctx", "head"),
            P("ctx", None),
            P("ctx", "head"),
            P("ctx", "head"),
        ),
        check_vma=False,
    )
```
